32 devices in a mesh: grp: 2 (over x), wide: 16 (over z, y, core).
Axes of the slice: x: 2, y: 2, z: 4, core: 2. Of those that a mesh axis runs over, the one named last changes fastest.
Arguments:
- slab: float32 [6, 2, 4096, 4096], P('grp', None, None, 'wide'), parts along dimension 0, may hold values from -6 to 6
- factor: float32 [4096, 256], P('wide'), may hold values from -0.09375 to 0.09375
Outputs:
- gram: float32 [8192, 4096], P(('grp', 'wide')), parts along dimension 0
The draws below stay inside these ranges and needn't reach their ends.
There are 2 independent parts, one for each index of `grp`. The reference program is written for one: setup_inputs(seed, part) draws one part's arguments, and reference() takes and returns one part's arrays. A program takes and returns all parts, laid end to end along the dimension named above; an argument that names none is the same for every part. Nothing has to cross between parts.
All inputs are finite; a program needn't handle non-finite values.
Results may differ from the reference program's by a relative error of at most 0.0034.
Values may be sent and summed in bfloat16 or wider, within the bound.
A program may use at most 128 MiB of HBM per device.

```python
import jax
import jax.numpy as jnp
from jax import lax

N1 = 4096
N2 = 4096
R2 = 256
PLANES = 3
VARS = 2


def block_scale(key, extent, split, low, top_value):
    gain = 1.0
    for axis_at, parts in split:
        heights = jax.random.uniform(jax.random.fold_in(jax.random.fold_in(key, 6), axis_at), (parts,), jnp.float32, low / len(split), top_value / len(split))
        gain = gain * jnp.repeat(jnp.exp(heights), extent[axis_at] // parts).reshape((-1,) + (1,) * (len(extent) - 1 - axis_at))
    return gain


def centred(own_key, dims, scale, most, shards=(), held_as=jnp.bfloat16):
    values = scale * jax.random.normal(own_key, dims, jnp.float32)
    if shards:
        values = values * block_scale(own_key, dims, shards, -0.22, 0.18)
    return jnp.clip(values, -most, most).astype(held_as)


def setup_inputs(seed: int = 0, part: int = 0) -> dict:
    streams_of = jax.random.split(jax.random.key(seed), 3)
    part_keys = jax.random.split(jax.random.fold_in(streams_of[2], part), 3)
    return {
        "slab": centred(part_keys[0], (PLANES, VARS, N1, N2), 1.0, 6.0, ((3, 16),), jnp.float32),
        "factor": centred(streams_of[1], (N2, R2), N2 ** -0.5, 0.09375, ((0, 16),), jnp.float32),
    }


def reference(slab, factor):
    projected = jnp.einsum("pvin,nr->ipvr", slab, factor, precision=lax.Precision.HIGHEST)
    projected = projected.reshape(slab.shape[2], -1).astype(jnp.bfloat16)
    width = projected.shape[1]
    gram = lax.dot_general(projected, projected, (((1,), (1,)), ((), ())), preferred_element_type=jnp.float32)
    return gram / float(width)
```

```python
import functools

import jax
import jax.numpy as jnp
from jax import lax
from jax.experimental import pallas as pl
from jax.experimental.pallas import tpu as pltpu
from jax.sharding import PartitionSpec as P

HALVES = 2


def narrow_hops(chips):
    hops = 0
    while 8 * (hops + 1) * (hops + 2) // 2 <= 3 * chips:
        hops += 1
    return hops


def kernel(
    chips, lanes, narrow, scale,
    slab, factor, gram,
    fsplit, fields, stage, sib, ring, narrow_out, narrow_in, held, gram_out, gram_in,
    field_sem, sib_send, sib_recv, hop_send, hop_recv, gather_send, gather_recv, gram_send, gram_recv,
):
    own_planes, rows = ring.shape[1], ring.shape[2]
    part = rows // HALVES
    me = lax.axis_index("wide")
    chip, core = lax.div(me, HALVES), lax.rem(me, HALVES)
    way = 1 - 2 * core

    def wrap(place):
        return lax.rem(place + 2 * chips, chips)

    def chip_at(place):
        if lanes == 1:
            return place
        lane = lax.div(place, chips // 2)
        return 2 * (place + lane * (chips - 1 - 2 * place)) + lane

    if lanes == 1:
        place = chip
    else:
        level, lane = lax.div(chip, 2), lax.rem(chip, 2)
        place = level + lane * (chips - 1 - 2 * level)

    after = {"wide": chip_at(wrap(place + way)) * HALVES + core}
    before = {"wide": chip_at(wrap(place - way)) * HALVES + core}
    sibling = {"wide": chip * HALVES + 1 - core}

    def fetch(step, which):
        towards = way if which == 0 else -way
        half = core if which == 0 else 1 - core
        first = pl.multiple_of(chip_at(wrap(place - towards * (1 + step))) * rows, rows)
        slot = lax.rem(step, 2)
        return pltpu.make_async_copy(
            slab.at[pl.ds(half * own_planes, own_planes), pl.ds(first, rows), :],
            fields.at[slot, which],
            field_sem.at[slot, which],
        )

    def remote(src, dst, send, recv, to):
        return pltpu.make_async_remote_copy(
            src_ref=src, dst_ref=dst, send_sem=send, recv_sem=recv,
            device_id=to, device_id_type=pl.DeviceIdType.MESH,
        )

    def to_sibling(step, j):
        slot = lax.rem(step, 2)
        return remote(stage.at[slot, j], sib.at[step, j], sib_send.at[slot, j], sib_recv.at[step, j], sibling)

    def wide_hop(step, j):
        return remote(ring.at[step - narrow, j], ring.at[step + 1 - narrow, j],
                      hop_send.at[step, j], hop_recv.at[step, j], after)

    def narrow_hop(step, j):
        return remote(narrow_out.at[step, j], narrow_in.at[step, j],
                      hop_send.at[step, j], hop_recv.at[step, j], after)

    def gather_hop(step, j):
        chunk = wrap(place - way * step)
        return remote(held.at[chunk, j], held.at[chunk, j],
                      gather_send.at[step, j], gather_recv.at[step, j], after)

    def gather_arrival(step, j):
        chunk = wrap(place - way * (step + 1))
        return remote(held.at[chunk, j], held.at[chunk, j],
                      gather_send.at[step, j], gather_recv.at[step, j], after)

    def gram_part(chunk):
        return remote(gram_out.at[chunk], gram_in.at[chunk], gram_send.at[chunk], gram_recv.at[chunk], sibling)

    def term(slot, which, j):
        x = fields[slot, which, j]
        high = x.astype(jnp.bfloat16)
        low = (x - high.astype(jnp.float32)).astype(jnp.bfloat16)
        dot = functools.partial(jnp.dot, preferred_element_type=jnp.float32)
        return dot(high, fsplit[0]) + (dot(high, fsplit[1]) + dot(low, fsplit[0]))

    def relay(step, reuse):
        fetch(step, 1).wait()
        slot = lax.rem(step, 2)

        def one(j, _):
            if reuse:
                to_sibling(step - 2, j).wait_send()
            stage[slot, j] = term(slot, 1, j)
            to_sibling(step, j).start()
            return _

        lax.fori_loop(0, own_planes, one, 0)

    def combine(step, kind_in, kind_out):
        fetch(step, 0).wait()
        slot = lax.rem(step, 2)

        def one(j, _):
            value = term(slot, 0, j)
            to_sibling(step, j).wait_recv()
            value = value + sib[step, j]
            if kind_in == "narrow":
                narrow_hop(step - 1, j).wait_recv()
                value = value + narrow_in[step - 1, j].astype(jnp.float32)
            elif kind_in == "wide":
                wide_hop(step - 1, j).wait_recv()
                value = value + ring[step - narrow, j]
            if kind_out == "narrow":
                narrow_out[step, j] = value.astype(jnp.bfloat16)
                narrow_hop(step, j).start()
            elif kind_out == "wide":
                ring[step - narrow, j] = value
                wide_hop(step, j).start()
            else:
                held[place, j] = value.astype(jnp.bfloat16)
                gather_hop(0, j).start()
            return _

        lax.fori_loop(0, own_planes, one, 0)

    def multiply(chunk):
        def rows_of(half):
            first = pl.multiple_of(half * part, part)
            total = None
            for j in range(own_planes):
                product = lax.dot_general(
                    held[place, j, pl.ds(first, part), :], held[chunk, j],
                    (((1,), (1,)), ((), ())), preferred_element_type=jnp.float32,
                )
                total = product if total is None else total + product
            return total

        gram_out[chunk] = rows_of(1 - core)
        gram_part(chunk).start()
        columns = pl.ds(pl.multiple_of(chip_at(chunk) * rows, rows), rows)
        gram[:, columns] = rows_of(core)

    for step in range(2):
        fetch(step, 1).start()
        fetch(step, 0).start()
    f = factor[...]
    fsplit[0] = f.astype(jnp.bfloat16)
    fsplit[1] = (f - f.astype(jnp.bfloat16).astype(jnp.float32)).astype(jnp.bfloat16)

    barrier = pltpu.get_barrier_semaphore()
    for other in (after, before, sibling):
        pl.semaphore_signal(barrier, inc=1, device_id=other, device_id_type=pl.DeviceIdType.MESH)
    pl.semaphore_wait(barrier, 3)

    relay(0, False)
    for step in range(narrow + 1):
        kind_in = None if step == 0 else "narrow"
        combine(step, kind_in, "narrow" if step < narrow else "wide")
        relay(step + 1, step + 1 >= 2)
        fetch(step + 2, 1).start()
        fetch(step + 2, 0).start()

    def middle(step, _):
        combine(step, "wide", "wide")
        relay(step + 1, True)

        @pl.when(step + 2 < chips)
        def _fetch():
            fetch(step + 2, 1).start()
            fetch(step + 2, 0).start()

        return _

    lax.fori_loop(narrow + 1, chips - 1, middle, 0)
    combine(chips - 1, "wide", "held")
    multiply(place)

    def gathered(step, _):
        def one(j, _):
            gather_arrival(step - 1, j).wait_recv()

            @pl.when(step < chips - 1)
            def _pass_on():
                gather_hop(step, j).start()

            return _

        lax.fori_loop(0, own_planes, one, 0)
        multiply(wrap(place - way * step))
        return _

    lax.fori_loop(1, chips, gathered, 0)

    def finish(chunk, _):
        gram_part(chunk).wait()
        columns = pl.ds(pl.multiple_of(chip_at(chunk) * rows, rows), rows)
        gram[:, columns] = (gram[:, columns] + gram_in[chunk]) * scale
        return _

    lax.fori_loop(0, chips, finish, 0)

    def drain(j, _):
        to_sibling(chips - 2, j).wait_send()
        to_sibling(chips - 1, j).wait_send()
        for step in range(narrow):
            narrow_hop(step, j).wait_send()

        def hop(step, _):
            wide_hop(step, j).wait_send()
            return _

        lax.fori_loop(narrow, chips - 1, hop, 0)

        def gather(step, _):
            gather_hop(step, j).wait_send()
            return _

        lax.fori_loop(0, chips - 1, gather, 0)
        return _

    lax.fori_loop(0, own_planes, drain, 0)


def shards(lanes, slab, factor):
    planes = slab.shape[0] * slab.shape[1]
    total_rows, depth = slab.shape[2:]
    ranks = factor.shape[1]
    devices = lax.axis_size("wide")
    chips = devices // HALVES
    rows = total_rows // chips
    own = planes // HALVES
    narrow = narrow_hops(chips)
    f32, bf16 = jnp.float32, jnp.bfloat16
    block = (own, rows, ranks)
    dma = pltpu.SemaphoreType.DMA
    return pl.pallas_call(
        functools.partial(kernel, chips, lanes, narrow, 1.0 / float(planes * ranks)),
        out_shape=jax.ShapeDtypeStruct((total_rows // devices, total_rows), f32),
        in_specs=[pl.BlockSpec(memory_space=pl.ANY), pl.BlockSpec(memory_space=pltpu.VMEM)],
        out_specs=pl.BlockSpec(memory_space=pltpu.VMEM),
        scratch_shapes=[
            pltpu.VMEM((2, depth, ranks), bf16),
            pltpu.VMEM((2, 2, own, rows, depth), f32),
            pltpu.VMEM((2,) + block, f32),
            pltpu.VMEM((chips,) + block, f32),
            pltpu.VMEM((chips - narrow,) + block, f32),
            pltpu.VMEM((max(narrow, 1),) + block, bf16),
            pltpu.VMEM((max(narrow, 1),) + block, bf16),
            pltpu.VMEM((chips,) + block, bf16),
            pltpu.VMEM((chips, rows // HALVES, rows), f32),
            pltpu.VMEM((chips, rows // HALVES, rows), f32),
            dma((2, 2)),
            dma((2, own)),
            dma((chips, own)),
            dma((chips - 1, own)),
            dma((chips - 1, own)),
            dma((chips - 1, own)),
            dma((chips - 1, own)),
            dma((chips,)),
            dma((chips,)),
        ],
        compiler_params=pltpu.CompilerParams(
            collective_id=0, has_side_effects=True, vmem_limit_bytes=60 * 2**20
        ),
        cost_estimate=pl.CostEstimate(
            flops=8 * planes * total_rows * depth * ranks, bytes_accessed=4 * slab.size, transcendentals=0
        ),
    )(slab.reshape(planes, total_rows, depth), factor)


def solution(mesh):
    lanes = 2 if mesh.shape["grp"] == 2 else 1
    placed = (P("grp", None, None, "wide"), P("wide", None))
    return jax.shard_map(
        functools.partial(shards, lanes),
        mesh=mesh, in_specs=placed, out_specs=P(("grp", "wide"), None), check_vma=False,
    )
```

```python
import functools

import jax
import jax.numpy as jnp
from jax import lax
from jax.experimental import pallas as pl
from jax.experimental.pallas import tpu as pltpu
from jax.sharding import PartitionSpec as P

HALVES = 2


SPAN = 83.0
PEAK_ROWS = 16


def encode(value, code):
    rows = value.shape[0]
    peak = jnp.maximum(jnp.max(jnp.abs(value), axis=0, keepdims=True), 1e-30).astype(jnp.bfloat16)
    wide_peak = peak.astype(jnp.float32)
    code[pl.ds(0, rows), :] = jnp.exp(value * (SPAN / wide_peak)).astype(jnp.bfloat16)
    code[pl.ds(rows, PEAK_ROWS), :] = jnp.broadcast_to(wide_peak, (PEAK_ROWS, value.shape[1])).astype(jnp.bfloat16)


def decode(code):
    rows = code.shape[0] - PEAK_ROWS
    peak = code[pl.ds(rows, PEAK_ROWS), :].astype(jnp.float32)[:1]
    return jnp.log(code[pl.ds(0, rows), :].astype(jnp.float32)) * (peak / SPAN)


def kernel(
    chips, lanes, scale,
    slab, factor, gram,
    fsplit, fields, stage, sib, code_out, code_in, held, gram_out, gram_in,
    field_sem, sib_send, sib_recv, hop_send, hop_recv, gather_send, gather_recv, gram_send, gram_recv,
):
    own_planes, rows = sib.shape[1], sib.shape[2]
    part = rows // HALVES
    me = lax.axis_index("wide")
    chip, core = lax.div(me, HALVES), lax.rem(me, HALVES)
    way = 1 - 2 * core

    def wrap(place):
        return lax.rem(place + 2 * chips, chips)

    def chip_at(place):
        if lanes == 1:
            return place
        lane = lax.div(place, chips // 2)
        return 2 * (place + lane * (chips - 1 - 2 * place)) + lane

    if lanes == 1:
        place = chip
    else:
        level, lane = lax.div(chip, 2), lax.rem(chip, 2)
        place = level + lane * (chips - 1 - 2 * level)

    after = {"wide": chip_at(wrap(place + way)) * HALVES + core}
    before = {"wide": chip_at(wrap(place - way)) * HALVES + core}
    sibling = {"wide": chip * HALVES + 1 - core}

    def fetch(step, which):
        towards = way if which == 0 else -way
        half = core if which == 0 else 1 - core
        first = pl.multiple_of(chip_at(wrap(place - towards * (1 + step))) * rows, rows)
        slot = lax.rem(step, 2)
        return pltpu.make_async_copy(
            slab.at[pl.ds(half * own_planes, own_planes), pl.ds(first, rows), :],
            fields.at[slot, which],
            field_sem.at[slot, which],
        )

    def remote(src, dst, send, recv, to):
        return pltpu.make_async_remote_copy(
            src_ref=src, dst_ref=dst, send_sem=send, recv_sem=recv,
            device_id=to, device_id_type=pl.DeviceIdType.MESH,
        )

    def to_sibling(step, j):
        slot = lax.rem(step, 2)
        return remote(stage.at[slot, j], sib.at[step, j], sib_send.at[slot, j], sib_recv.at[step, j], sibling)

    def hop(step, j):
        return remote(code_out.at[step, j], code_in.at[step, j],
                      hop_send.at[step, j], hop_recv.at[step, j], after)

    def gather_hop(step, j):
        chunk = wrap(place - way * step)
        return remote(held.at[chunk, j], held.at[chunk, j],
                      gather_send.at[step, j], gather_recv.at[step, j], after)

    def gather_arrival(step, j):
        chunk = wrap(place - way * (step + 1))
        return remote(held.at[chunk, j], held.at[chunk, j],
                      gather_send.at[step, j], gather_recv.at[step, j], after)

    def gram_part(chunk):
        return remote(gram_out.at[chunk], gram_in.at[chunk], gram_send.at[chunk], gram_recv.at[chunk], sibling)

    def term(slot, which, j):
        x = fields[slot, which, j]
        high = x.astype(jnp.bfloat16)
        low = (x - high.astype(jnp.float32)).astype(jnp.bfloat16)
        dot = functools.partial(jnp.dot, preferred_element_type=jnp.float32)
        return dot(high, fsplit[0]) + (dot(high, fsplit[1]) + dot(low, fsplit[0]))

    def relay(step, j, reuse):
        slot = lax.rem(step, 2)
        if reuse:
            to_sibling(step - 2, j).wait_send()
        stage[slot, j] = term(slot, 1, j)
        to_sibling(step, j).start()

    def combine(step, j, first, last):
        value = term(lax.rem(step, 2), 0, j)
        to_sibling(step, j).wait_recv()
        value = value + sib[step, j]
        if not first:
            hop(step - 1, j).wait_recv()
            value = value + decode(code_in.at[step - 1, j])
        if last:
            held[place, j] = value.astype(jnp.bfloat16)
            gather_hop(0, j).start()
        else:
            encode(value, code_out.at[step, j])
            hop(step, j).start()

    def each(body):
        def one(j, carry):
            body(j)
            return carry

        lax.fori_loop(0, own_planes, one, 0)

    def multiply(chunk):
        def rows_of(half):
            first = pl.multiple_of(half * part, part)
            total = None
            for j in range(own_planes):
                product = lax.dot_general(
                    held[place, j, pl.ds(first, part), :], held[chunk, j],
                    (((1,), (1,)), ((), ())), preferred_element_type=jnp.float32,
                )
                total = product if total is None else total + product
            return total

        gram_out[chunk] = rows_of(1 - core)
        gram_part(chunk).start()
        columns = pl.ds(pl.multiple_of(chip_at(chunk) * rows, rows), rows)
        gram[:, columns] = rows_of(core)

    for step in range(2):
        fetch(step, 1).start()
        fetch(step, 0).start()
    f = factor[...]
    fsplit[0] = f.astype(jnp.bfloat16)
    fsplit[1] = (f - f.astype(jnp.bfloat16).astype(jnp.float32)).astype(jnp.bfloat16)

    barrier = pltpu.get_barrier_semaphore()
    for other in (after, before, sibling):
        pl.semaphore_signal(barrier, inc=1, device_id=other, device_id_type=pl.DeviceIdType.MESH)
    pl.semaphore_wait(barrier, 3)

    fetch(0, 1).wait()
    relay(0, 0, False)
    fetch(0, 0).wait()
    for j in range(own_planes):
        if j + 1 < own_planes:
            relay(0, j + 1, False)
        combine(0, j, True, False)
    fetch(2, 1).start()
    fetch(2, 0).start()
    fetch(1, 1).wait()
    each(lambda j: relay(1, j, False))

    def middle(step, carry):
        fetch(step, 0).wait()
        each(lambda j: combine(step, j, False, False))

        @pl.when(step + 2 < chips)
        def _fetch():
            fetch(step + 2, 1).start()
            fetch(step + 2, 0).start()

        fetch(step + 1, 1).wait()
        each(lambda j: relay(step + 1, j, True))
        return carry

    lax.fori_loop(1, chips - 1, middle, 0)
    fetch(chips - 1, 0).wait()
    each(lambda j: combine(chips - 1, j, False, True))
    multiply(place)

    def gathered(step, _):
        def one(j, _):
            gather_arrival(step - 1, j).wait_recv()

            @pl.when(step < chips - 1)
            def _pass_on():
                gather_hop(step, j).start()

            return _

        lax.fori_loop(0, own_planes, one, 0)
        multiply(wrap(place - way * step))
        return _

    lax.fori_loop(1, chips, gathered, 0)

    def finish(chunk, _):
        gram_part(chunk).wait()
        columns = pl.ds(pl.multiple_of(chip_at(chunk) * rows, rows), rows)
        gram[:, columns] = (gram[:, columns] + gram_in[chunk]) * scale
        return _

    lax.fori_loop(0, chips, finish, 0)

    def drain(j, _):
        to_sibling(chips - 2, j).wait_send()
        to_sibling(chips - 1, j).wait_send()

        def sums(step, _):
            hop(step, j).wait_send()
            return _

        lax.fori_loop(0, chips - 1, sums, 0)

        def gather(step, _):
            gather_hop(step, j).wait_send()
            return _

        lax.fori_loop(0, chips - 1, gather, 0)
        return _

    lax.fori_loop(0, own_planes, drain, 0)


def shards(lanes, slab, factor):
    planes = slab.shape[0] * slab.shape[1]
    total_rows, depth = slab.shape[2:]
    ranks = factor.shape[1]
    devices = lax.axis_size("wide")
    chips = devices // HALVES
    rows = total_rows // chips
    own = planes // HALVES
    f32, bf16 = jnp.float32, jnp.bfloat16
    block = (own, rows, ranks)
    dma = pltpu.SemaphoreType.DMA
    return pl.pallas_call(
        functools.partial(kernel, chips, lanes, 1.0 / float(planes * ranks)),
        out_shape=jax.ShapeDtypeStruct((total_rows // devices, total_rows), f32),
        in_specs=[pl.BlockSpec(memory_space=pl.ANY), pl.BlockSpec(memory_space=pltpu.VMEM)],
        out_specs=pl.BlockSpec(memory_space=pltpu.VMEM),
        scratch_shapes=[
            pltpu.VMEM((2, depth, ranks), bf16),
            pltpu.VMEM((2, 2, own, rows, depth), f32),
            pltpu.VMEM((2,) + block, f32),
            pltpu.VMEM((chips,) + block, f32),
            pltpu.VMEM((chips - 1, own, rows + PEAK_ROWS, ranks), bf16),
            pltpu.VMEM((chips - 1, own, rows + PEAK_ROWS, ranks), bf16),
            pltpu.VMEM((chips,) + block, bf16),
            pltpu.VMEM((chips, rows // HALVES, rows), f32),
            pltpu.VMEM((chips, rows // HALVES, rows), f32),
            dma((2, 2)),
            dma((2, own)),
            dma((chips, own)),
            dma((chips - 1, own)),
            dma((chips - 1, own)),
            dma((chips - 1, own)),
            dma((chips - 1, own)),
            dma((chips,)),
            dma((chips,)),
        ],
        compiler_params=pltpu.CompilerParams(
            collective_id=0, has_side_effects=True, vmem_limit_bytes=60 * 2**20
        ),
        cost_estimate=pl.CostEstimate(
            flops=8 * planes * total_rows * depth * ranks, bytes_accessed=4 * slab.size, transcendentals=0
        ),
    )(slab.reshape(planes, total_rows, depth), factor)


def solution(mesh):
    lanes = 2 if mesh.shape["grp"] == 2 else 1
    placed = (P("grp", None, None, "wide"), P("wide", None))
    return jax.shard_map(
        functools.partial(shards, lanes),
        mesh=mesh, in_specs=placed, out_specs=P(("grp", "wide"), None), check_vma=False,
    )
```

```python
import functools

import jax
import jax.numpy as jnp
from jax import lax
from jax.experimental import pallas as pl
from jax.experimental.pallas import tpu as pltpu
from jax.sharding import PartitionSpec as P

HALVES = 2


SPAN = 83.0
PEAK_ROWS = 16


def encode(value, code):
    rows = value.shape[0]
    peak = jnp.maximum(jnp.max(jnp.abs(value), axis=0, keepdims=True), 1e-30).astype(jnp.bfloat16)
    wide_peak = peak.astype(jnp.float32)
    code[pl.ds(0, rows), :] = jnp.exp(value * (SPAN / wide_peak)).astype(jnp.bfloat16)
    code[pl.ds(rows, PEAK_ROWS), :] = jnp.broadcast_to(wide_peak, (PEAK_ROWS, value.shape[1])).astype(jnp.bfloat16)


def decode(code):
    rows = code.shape[0] - PEAK_ROWS
    peak = code[pl.ds(rows, PEAK_ROWS), :].astype(jnp.float32)[:1]
    return jnp.log(code[pl.ds(0, rows), :].astype(jnp.float32)) * (peak / SPAN)


def kernel(
    chips, lanes, scale,
    slab, factor, gram,
    fsplit, fields, stage, sib, code_out, code_in, held, gram_out, gram_in,
    field_sem, sib_send, sib_recv, hop_send, hop_recv, gather_send, gather_recv, gram_send, gram_recv,
):
    own_planes, rows = sib.shape[1], sib.shape[2]
    part = rows // HALVES
    me = lax.axis_index("wide")
    chip, core = lax.div(me, HALVES), lax.rem(me, HALVES)
    way = 1 - 2 * core

    def wrap(place):
        return lax.rem(place + 2 * chips, chips)

    def chip_at(place):
        if lanes == 1:
            return place
        lane = lax.div(place, chips // 2)
        return 2 * (place + lane * (chips - 1 - 2 * place)) + lane

    if lanes == 1:
        place = chip
    else:
        level, lane = lax.div(chip, 2), lax.rem(chip, 2)
        place = level + lane * (chips - 1 - 2 * level)

    after = {"wide": chip_at(wrap(place + way)) * HALVES + core}
    before = {"wide": chip_at(wrap(place - way)) * HALVES + core}
    sibling = {"wide": chip * HALVES + 1 - core}

    def fetch(step, which):
        towards = way if which == 0 else -way
        half = core if which == 0 else 1 - core
        first = pl.multiple_of(chip_at(wrap(place - towards * (1 + step))) * rows, rows)
        slot = lax.rem(step, 2)
        return pltpu.make_async_copy(
            slab.at[pl.ds(half * own_planes, own_planes), pl.ds(first, rows), :],
            fields.at[slot, which],
            field_sem.at[slot, which],
        )

    def remote(src, dst, send, recv, to):
        return pltpu.make_async_remote_copy(
            src_ref=src, dst_ref=dst, send_sem=send, recv_sem=recv,
            device_id=to, device_id_type=pl.DeviceIdType.MESH,
        )

    def to_sibling(step, j):
        slot = lax.rem(step, 2)
        return remote(stage.at[slot, j], sib.at[step, j], sib_send.at[slot, j], sib_recv.at[step, j], sibling)

    def hop(step, j):
        return remote(code_out.at[step, j], code_in.at[step, j],
                      hop_send.at[step, j], hop_recv.at[step, j], after)

    def gather_hop(step, j):
        chunk = wrap(place - way * step)
        return remote(held.at[chunk, j], held.at[chunk, j],
                      gather_send.at[step, j], gather_recv.at[step, j], after)

    def gather_arrival(step, j):
        chunk = wrap(place - way * (step + 1))
        return remote(held.at[chunk, j], held.at[chunk, j],
                      gather_send.at[step, j], gather_recv.at[step, j], after)

    def gram_part(chunk):
        return remote(gram_out.at[chunk], gram_in.at[chunk], gram_send.at[chunk], gram_recv.at[chunk], sibling)

    def term(slot, which, j):
        x = fields[slot, which, j]
        high = x.astype(jnp.bfloat16)
        low = (x - high.astype(jnp.float32)).astype(jnp.bfloat16)
        dot = functools.partial(jnp.dot, preferred_element_type=jnp.float32)
        return dot(high, fsplit[0]) + (dot(high, fsplit[1]) + dot(low, fsplit[0]))

    def relay(step, j, reuse):
        slot = lax.rem(step, 2)
        if reuse:
            to_sibling(step - 2, j).wait_send()
        stage[slot, j] = term(slot, 1, j)
        to_sibling(step, j).start()

    def combine(step, j, first, last):
        value = term(lax.rem(step, 2), 0, j)
        to_sibling(step, j).wait_recv()
        value = value + sib[step, j]
        if not first:
            hop(step - 1, j).wait_recv()
            value = value + decode(code_in.at[step - 1, j])
        if last:
            held[place, j] = value.astype(jnp.bfloat16)
            gather_hop(0, j).start()
        else:
            encode(value, code_out.at[step, j])
            hop(step, j).start()

    def each(body):
        def one(j, carry):
            body(j)
            return carry

        lax.fori_loop(0, own_planes, one, 0)

    def multiply(chunk):
        def rows_of(half):
            first = pl.multiple_of(half * part, part)
            total = None
            for j in range(own_planes):
                product = lax.dot_general(
                    held[place, j, pl.ds(first, part), :], held[chunk, j],
                    (((1,), (1,)), ((), ())), preferred_element_type=jnp.float32,
                )
                total = product if total is None else total + product
            return total * scale

        gram_out[chunk] = rows_of(1 - core)
        gram_part(chunk).start()
        columns = pl.ds(pl.multiple_of(chip_at(chunk) * rows, rows), rows)
        gram[:, columns] = rows_of(core)

    for step in range(2):
        fetch(step, 1).start()
        fetch(step, 0).start()
    f = factor[...]
    fsplit[0] = f.astype(jnp.bfloat16)
    fsplit[1] = (f - f.astype(jnp.bfloat16).astype(jnp.float32)).astype(jnp.bfloat16)

    barrier = pltpu.get_barrier_semaphore()
    for other in (after, before, sibling):
        pl.semaphore_signal(barrier, inc=1, device_id=other, device_id_type=pl.DeviceIdType.MESH)
    pl.semaphore_wait(barrier, 3)

    fetch(0, 1).wait()
    relay(0, 0, False)
    fetch(0, 0).wait()
    for j in range(own_planes):
        if j + 1 < own_planes:
            relay(0, j + 1, False)
        combine(0, j, True, False)
    fetch(2, 1).start()
    fetch(2, 0).start()
    fetch(1, 1).wait()
    each(lambda j: relay(1, j, False))

    def middle(step, carry):
        fetch(step, 0).wait()
        fetch(step + 1, 1).wait()

        def both(j):
            combine(step, j, False, False)
            relay(step + 1, j, True)

        each(both)

        @pl.when(step + 2 < chips)
        def _fetch():
            fetch(step + 2, 1).start()
            fetch(step + 2, 0).start()

        return carry

    lax.fori_loop(1, chips - 1, middle, 0)
    fetch(chips - 1, 0).wait()
    each(lambda j: combine(chips - 1, j, False, True))
    multiply(place)

    def finish(chunk):
        gram_part(chunk).wait_recv()
        columns = pl.ds(pl.multiple_of(chip_at(chunk) * rows, rows), rows)
        gram[:, columns] += gram_in[chunk]

    def gathered(step, carry):
        def arrive(j):
            gather_arrival(step - 1, j).wait_recv()

            @pl.when(step < chips - 1)
            def _pass_on():
                gather_hop(step, j).start()

        each(arrive)
        multiply(wrap(place - way * step))

        @pl.when(step == chips // 2)
        def _first():
            finish(place)

        @pl.when(step > chips // 2)
        def _met():
            finish(wrap(place - way * step))
            finish(wrap(place - way * (chips - step + 1)))

        return carry

    lax.fori_loop(1, chips, gathered, 0)
    finish(wrap(place - way))

    def drain_gram(chunk, carry):
        gram_part(chunk).wait_send()
        return carry

    lax.fori_loop(0, chips, drain_gram, 0)

    def drain(j, _):
        to_sibling(chips - 2, j).wait_send()
        to_sibling(chips - 1, j).wait_send()

        def sums(step, _):
            hop(step, j).wait_send()
            return _

        lax.fori_loop(0, chips - 1, sums, 0)

        def gather(step, _):
            gather_hop(step, j).wait_send()
            return _

        lax.fori_loop(0, chips - 1, gather, 0)
        return _

    lax.fori_loop(0, own_planes, drain, 0)


def shards(lanes, slab, factor):
    planes = slab.shape[0] * slab.shape[1]
    total_rows, depth = slab.shape[2:]
    ranks = factor.shape[1]
    devices = lax.axis_size("wide")
    chips = devices // HALVES
    rows = total_rows // chips
    own = planes // HALVES
    f32, bf16 = jnp.float32, jnp.bfloat16
    block = (own, rows, ranks)
    dma = pltpu.SemaphoreType.DMA
    return pl.pallas_call(
        functools.partial(kernel, chips, lanes, 1.0 / float(planes * ranks)),
        out_shape=pltpu.VMEM((total_rows // devices, total_rows), f32),
        in_specs=[pl.BlockSpec(memory_space=pl.ANY), pl.BlockSpec(memory_space=pltpu.VMEM)],
        out_specs=pl.BlockSpec(memory_space=pltpu.VMEM),
        scratch_shapes=[
            pltpu.VMEM((2, depth, ranks), bf16),
            pltpu.VMEM((2, 2, own, rows, depth), f32),
            pltpu.VMEM((2,) + block, f32),
            pltpu.VMEM((chips,) + block, f32),
            pltpu.VMEM((chips - 1, own, rows + PEAK_ROWS, ranks), bf16),
            pltpu.VMEM((chips - 1, own, rows + PEAK_ROWS, ranks), bf16),
            pltpu.VMEM((chips,) + block, bf16),
            pltpu.VMEM((chips, rows // HALVES, rows), f32),
            pltpu.VMEM((chips, rows // HALVES, rows), f32),
            dma((2, 2)),
            dma((2, own)),
            dma((chips, own)),
            dma((chips - 1, own)),
            dma((chips - 1, own)),
            dma((chips - 1, own)),
            dma((chips - 1, own)),
            dma((chips,)),
            dma((chips,)),
        ],
        compiler_params=pltpu.CompilerParams(
            collective_id=0, has_side_effects=True, vmem_limit_bytes=54 * 2**20
        ),
        cost_estimate=pl.CostEstimate(
            flops=8 * planes * total_rows * depth * ranks, bytes_accessed=4 * slab.size, transcendentals=0
        ),
    )(slab.reshape(planes, total_rows, depth), factor)


def solution(mesh):
    lanes = 2 if mesh.shape["grp"] == 2 else 1
    placed = (P("grp", None, None, "wide"), P("wide", None))
    return jax.shard_map(
        functools.partial(shards, lanes),
        mesh=mesh, in_specs=placed, out_specs=P(("grp", "wide"), None), check_vma=False,
    )
```

```python
import functools

import jax
import jax.numpy as jnp
from jax import lax
from jax.experimental import pallas as pl
from jax.experimental.pallas import tpu as pltpu
from jax.sharding import PartitionSpec as P

HALVES = 2


SPAN = 83.0
PEAK_ROWS = 16


def encode(value, code):
    rows = value.shape[0]
    peak = jnp.maximum(jnp.max(jnp.abs(value), axis=0, keepdims=True), 1e-30).astype(jnp.bfloat16)
    wide_peak = peak.astype(jnp.float32)
    code[pl.ds(0, rows), :] = jnp.exp(value * (SPAN / wide_peak)).astype(jnp.bfloat16)
    code[pl.ds(rows, PEAK_ROWS), :] = jnp.broadcast_to(wide_peak, (PEAK_ROWS, value.shape[1])).astype(jnp.bfloat16)


def decode(code):
    rows = code.shape[0] - PEAK_ROWS
    peak = code[pl.ds(rows, PEAK_ROWS), :].astype(jnp.float32)[:1]
    return jnp.log(code[pl.ds(0, rows), :].astype(jnp.float32)) * (peak / SPAN)


def kernel(
    chips, lanes, scale,
    slab, factor, gram,
    fsplit, fields, stage, sib, code_out, code_in, held, gram_out, gram_in,
    field_sem, sib_send, sib_recv, hop_send, hop_recv, gather_send, gather_recv, gram_send, gram_recv,
):
    own_planes, rows = sib.shape[1], sib.shape[2]
    part = rows // HALVES
    me = lax.axis_index("wide")
    chip, core = lax.div(me, HALVES), lax.rem(me, HALVES)
    way = 1 - 2 * core

    def wrap(place):
        return lax.rem(place + 2 * chips, chips)

    def chip_at(place):
        if lanes == 1:
            return place
        lane = lax.div(place, chips // 2)
        return 2 * (place + lane * (chips - 1 - 2 * place)) + lane

    if lanes == 1:
        place = chip
    else:
        level, lane = lax.div(chip, 2), lax.rem(chip, 2)
        place = level + lane * (chips - 1 - 2 * level)

    after = {"wide": chip_at(wrap(place + way)) * HALVES + core}
    before = {"wide": chip_at(wrap(place - way)) * HALVES + core}
    sibling = {"wide": chip * HALVES + 1 - core}

    def fetch(step, which):
        towards = way if which == 0 else -way
        half = core if which == 0 else 1 - core
        first = pl.multiple_of(chip_at(wrap(place - towards * (1 + step))) * rows, rows)
        slot = lax.rem(step, 2)
        return pltpu.make_async_copy(
            slab.at[pl.ds(half * own_planes, own_planes), pl.ds(first, rows), :],
            fields.at[slot, which],
            field_sem.at[slot, which],
        )

    def remote(src, dst, send, recv, to):
        return pltpu.make_async_remote_copy(
            src_ref=src, dst_ref=dst, send_sem=send, recv_sem=recv,
            device_id=to, device_id_type=pl.DeviceIdType.MESH,
        )

    def to_sibling(step, j):
        slot = lax.rem(step, 2)
        return remote(stage.at[slot, j], sib.at[step, j], sib_send.at[slot, j], sib_recv.at[step, j], sibling)

    def hop(step, j):
        return remote(code_out.at[step, j], code_in.at[step, j],
                      hop_send.at[step, j], hop_recv.at[step, j], after)

    def gather_hop(step, j):
        chunk = wrap(place - way * step)
        return remote(held.at[chunk, j], held.at[chunk, j],
                      gather_send.at[step, j], gather_recv.at[step, j], after)

    def gather_arrival(step, j):
        chunk = wrap(place - way * (step + 1))
        return remote(held.at[chunk, j], held.at[chunk, j],
                      gather_send.at[step, j], gather_recv.at[step, j], after)

    def gram_part(chunk):
        return remote(gram_out.at[chunk], gram_in.at[chunk], gram_send.at[chunk], gram_recv.at[chunk], sibling)

    def term(slot, which, j):
        x = fields[slot, which, j]
        high = x.astype(jnp.bfloat16)
        low = (x - high.astype(jnp.float32)).astype(jnp.bfloat16)
        dot = functools.partial(jnp.dot, preferred_element_type=jnp.float32)
        return dot(high, fsplit[0]) + (dot(high, fsplit[1]) + dot(low, fsplit[0]))

    def prepare(step, j):
        slot = lax.rem(step, 2)
        stage[slot, j] = term(slot, 1, j)

    def relay(step, j, reuse):
        if reuse:
            to_sibling(step - 2, j).wait_send()
        prepare(step, j)
        to_sibling(step, j).start()

    def combine(step, j, first, last):
        value = term(lax.rem(step, 2), 0, j)
        to_sibling(step, j).wait_recv()
        value = value + sib[step, j]
        if not first:
            hop(step - 1, j).wait_recv()
            value = value + decode(code_in.at[step - 1, j])
        if last:
            held[place, j] = value.astype(jnp.bfloat16)
            gather_hop(0, j).start()
        else:
            encode(value, code_out.at[step, j])
            hop(step, j).start()

    def each(body):
        def one(j, carry):
            body(j)
            return carry

        lax.fori_loop(0, own_planes, one, 0)

    def multiply(chunk):
        def rows_of(half):
            first = pl.multiple_of(half * part, part)
            total = None
            for j in range(own_planes):
                product = lax.dot_general(
                    held[place, j, pl.ds(first, part), :], held[chunk, j],
                    (((1,), (1,)), ((), ())), preferred_element_type=jnp.float32,
                )
                total = product if total is None else total + product
            return total * scale

        gram_out[chunk] = rows_of(1 - core)
        gram_part(chunk).start()
        columns = pl.ds(pl.multiple_of(chip_at(chunk) * rows, rows), rows)
        gram[:, columns] = rows_of(core)

    for step in range(2):
        fetch(step, 1).start()
        fetch(step, 0).start()
    f = factor[...]
    fsplit[0] = f.astype(jnp.bfloat16)
    fsplit[1] = (f - f.astype(jnp.bfloat16).astype(jnp.float32)).astype(jnp.bfloat16)

    barrier = pltpu.get_barrier_semaphore()
    for other in (after, before, sibling):
        pl.semaphore_signal(barrier, inc=1, device_id=other, device_id_type=pl.DeviceIdType.MESH)
    fetch(0, 1).wait()
    each(lambda j: prepare(0, j))
    pl.semaphore_wait(barrier, 3)

    each(lambda j: to_sibling(0, j).start())
    fetch(0, 0).wait()
    each(lambda j: combine(0, j, True, False))
    fetch(2, 1).start()
    fetch(2, 0).start()
    fetch(1, 1).wait()
    each(lambda j: relay(1, j, False))

    def middle(step, carry):
        fetch(step, 0).wait()
        fetch(step + 1, 1).wait()

        def both(j):
            combine(step, j, False, False)
            relay(step + 1, j, True)

        each(both)

        @pl.when(step + 2 < chips)
        def _fetch():
            fetch(step + 2, 1).start()
            fetch(step + 2, 0).start()

        return carry

    lax.fori_loop(1, chips - 1, middle, 0)
    fetch(chips - 1, 0).wait()
    each(lambda j: combine(chips - 1, j, False, True))
    multiply(place)

    def finish(chunk):
        gram_part(chunk).wait_recv()
        columns = pl.ds(pl.multiple_of(chip_at(chunk) * rows, rows), rows)
        gram[:, columns] += gram_in[chunk]

    def gathered(step, carry):
        def arrive(j):
            gather_arrival(step - 1, j).wait_recv()

            @pl.when(step < chips - 1)
            def _pass_on():
                gather_hop(step, j).start()

        each(arrive)
        multiply(wrap(place - way * step))

        @pl.when(step == chips // 2)
        def _first():
            finish(place)

        @pl.when(step > chips // 2)
        def _met():
            finish(wrap(place - way * step))
            finish(wrap(place - way * (chips - step + 1)))

        return carry

    lax.fori_loop(1, chips, gathered, 0)
    finish(wrap(place - way))

    def drain_gram(chunk, carry):
        gram_part(chunk).wait_send()
        return carry

    lax.fori_loop(0, chips, drain_gram, 0)

    def drain(j, _):
        to_sibling(chips - 2, j).wait_send()
        to_sibling(chips - 1, j).wait_send()

        def sums(step, _):
            hop(step, j).wait_send()
            return _

        lax.fori_loop(0, chips - 1, sums, 0)

        def gather(step, _):
            gather_hop(step, j).wait_send()
            return _

        lax.fori_loop(0, chips - 1, gather, 0)
        return _

    lax.fori_loop(0, own_planes, drain, 0)


def shards(lanes, slab, factor):
    planes = slab.shape[0] * slab.shape[1]
    total_rows, depth = slab.shape[2:]
    ranks = factor.shape[1]
    devices = lax.axis_size("wide")
    chips = devices // HALVES
    rows = total_rows // chips
    own = planes // HALVES
    f32, bf16 = jnp.float32, jnp.bfloat16
    block = (own, rows, ranks)
    dma = pltpu.SemaphoreType.DMA
    return pl.pallas_call(
        functools.partial(kernel, chips, lanes, 1.0 / float(planes * ranks)),
        out_shape=pltpu.VMEM((total_rows // devices, total_rows), f32),
        in_specs=[pl.BlockSpec(memory_space=pl.ANY), pl.BlockSpec(memory_space=pltpu.VMEM)],
        out_specs=pl.BlockSpec(memory_space=pltpu.VMEM),
        scratch_shapes=[
            pltpu.VMEM((2, depth, ranks), bf16),
            pltpu.VMEM((2, 2, own, rows, depth), f32),
            pltpu.VMEM((2,) + block, f32),
            pltpu.VMEM((chips,) + block, f32),
            pltpu.VMEM((chips - 1, own, rows + PEAK_ROWS, ranks), bf16),
            pltpu.VMEM((chips - 1, own, rows + PEAK_ROWS, ranks), bf16),
            pltpu.VMEM((chips,) + block, bf16),
            pltpu.VMEM((chips, rows // HALVES, rows), f32),
            pltpu.VMEM((chips, rows // HALVES, rows), f32),
            dma((2, 2)),
            dma((2, own)),
            dma((chips, own)),
            dma((chips - 1, own)),
            dma((chips - 1, own)),
            dma((chips - 1, own)),
            dma((chips - 1, own)),
            dma((chips,)),
            dma((chips,)),
        ],
        compiler_params=pltpu.CompilerParams(
            collective_id=0, has_side_effects=True, vmem_limit_bytes=54 * 2**20
        ),
        cost_estimate=pl.CostEstimate(
            flops=8 * planes * total_rows * depth * ranks, bytes_accessed=4 * slab.size, transcendentals=0
        ),
    )(slab.reshape(planes, total_rows, depth), factor)


def solution(mesh):
    lanes = 2 if mesh.shape["grp"] == 2 else 1
    placed = (P("grp", None, None, "wide"), P("wide", None))
    return jax.shard_map(
        functools.partial(shards, lanes),
        mesh=mesh, in_specs=placed, out_specs=P(("grp", "wide"), None), check_vma=False,
    )
```

```python
import functools

import jax
import jax.numpy as jnp
from jax import lax
from jax.experimental import pallas as pl
from jax.experimental.pallas import tpu as pltpu
from jax.sharding import PartitionSpec as P

HALVES = 2


SPAN = 83.0
PEAK_ROWS = 16


def encode(value, code):
    rows = value.shape[0]
    peak = jnp.maximum(jnp.max(jnp.abs(value), axis=0, keepdims=True), 1e-30).astype(jnp.bfloat16)
    wide_peak = peak.astype(jnp.float32)
    code[pl.ds(0, rows), :] = jnp.exp(value * (SPAN / wide_peak)).astype(jnp.bfloat16)
    code[pl.ds(rows, PEAK_ROWS), :] = jnp.broadcast_to(wide_peak, (PEAK_ROWS, value.shape[1])).astype(jnp.bfloat16)


def decode(code):
    rows = code.shape[0] - PEAK_ROWS
    peak = code[pl.ds(rows, PEAK_ROWS), :].astype(jnp.float32)[:1]
    return jnp.log(code[pl.ds(0, rows), :].astype(jnp.float32)) * (peak / SPAN)


def kernel(
    chips, lanes, scale,
    slab, factor, gram,
    fsplit, fields, stage, sib, code_out, code_in, held, gram_out, gram_in,
    field_sem, sib_send, sib_recv, hop_send, hop_recv, gather_send, gather_recv, gram_send, gram_recv,
):
    own_planes, rows = sib.shape[1], sib.shape[2]
    part = rows // HALVES
    me = lax.axis_index("wide")
    chip, core = lax.div(me, HALVES), lax.rem(me, HALVES)
    way = 1 - 2 * core

    def wrap(place):
        return lax.rem(place + 2 * chips, chips)

    def chip_at(place):
        if lanes == 1:
            return place
        lane = lax.div(place, chips // 2)
        return 2 * (place + lane * (chips - 1 - 2 * place)) + lane

    if lanes == 1:
        place = chip
    else:
        level, lane = lax.div(chip, 2), lax.rem(chip, 2)
        place = level + lane * (chips - 1 - 2 * level)

    after = {"wide": chip_at(wrap(place + way)) * HALVES + core}
    before = {"wide": chip_at(wrap(place - way)) * HALVES + core}
    sibling = {"wide": chip * HALVES + 1 - core}

    def fetch(step, which):
        towards = way if which == 0 else -way
        half = core if which == 0 else 1 - core
        first = pl.multiple_of(chip_at(wrap(place - towards * (1 + step))) * rows, rows)
        slot = lax.rem(step, 2)
        return pltpu.make_async_copy(
            slab.at[pl.ds(half * own_planes, own_planes), pl.ds(first, rows), :],
            fields.at[slot, which],
            field_sem.at[slot, which],
        )

    def remote(src, dst, send, recv, to):
        return pltpu.make_async_remote_copy(
            src_ref=src, dst_ref=dst, send_sem=send, recv_sem=recv,
            device_id=to, device_id_type=pl.DeviceIdType.MESH,
        )

    def to_sibling(step, j):
        slot = lax.rem(step, 2)
        return remote(stage.at[slot, j], sib.at[step, j], sib_send.at[slot, j], sib_recv.at[step, j], sibling)

    def hop(step, j):
        return remote(code_out.at[step, j], code_in.at[step, j],
                      hop_send.at[step, j], hop_recv.at[step, j], after)

    def gather_hop(step, j):
        chunk = wrap(place - way * step)
        return remote(held.at[chunk, j], held.at[chunk, j],
                      gather_send.at[step, j], gather_recv.at[step, j], after)

    def gather_arrival(step, j):
        chunk = wrap(place - way * (step + 1))
        return remote(held.at[chunk, j], held.at[chunk, j],
                      gather_send.at[step, j], gather_recv.at[step, j], after)

    def gram_part(chunk):
        return remote(gram_out.at[chunk], gram_in.at[chunk], gram_send.at[chunk], gram_recv.at[chunk], sibling)

    def term(slot, which, j):
        x = fields[slot, which, j]
        high = x.astype(jnp.bfloat16)
        low = (x - high.astype(jnp.float32)).astype(jnp.bfloat16)
        dot = functools.partial(jnp.dot, preferred_element_type=jnp.float32)
        return dot(high, fsplit[0]) + (dot(high, fsplit[1]) + dot(low, fsplit[0]))

    def relay(step, j, reuse):
        slot = lax.rem(step, 2)
        if reuse:
            to_sibling(step - 2, j).wait_send()
        stage[slot, j] = term(slot, 1, j)
        to_sibling(step, j).start()

    def combine(step, j, first, last):
        value = term(lax.rem(step, 2), 0, j)
        to_sibling(step, j).wait_recv()
        value = value + sib[step, j]
        if not first:
            hop(step - 1, j).wait_recv()
            value = value + decode(code_in.at[step - 1, j])
        if last:
            held[place, j] = value.astype(jnp.bfloat16)
            gather_hop(0, j).start()
        else:
            encode(value, code_out.at[step, j])
            hop(step, j).start()

    def each(body):
        def one(j, carry):
            body(j)
            return carry

        lax.fori_loop(0, own_planes, one, 0)

    def multiply(chunk):
        def rows_of(half):
            first = pl.multiple_of(half * part, part)
            total = None
            for j in range(own_planes):
                product = lax.dot_general(
                    held[place, j, pl.ds(first, part), :], held[chunk, j],
                    (((1,), (1,)), ((), ())), preferred_element_type=jnp.float32,
                )
                total = product if total is None else total + product
            return total * scale

        gram_out[chunk] = rows_of(1 - core)
        gram_part(chunk).start()
        columns = pl.ds(pl.multiple_of(chip_at(chunk) * rows, rows), rows)
        gram[:, columns] = rows_of(core)

    fetch(0, 1).start()
    fetch(0, 0).start()
    f = factor[...]
    fsplit[0] = f.astype(jnp.bfloat16)
    fsplit[1] = (f - f.astype(jnp.bfloat16).astype(jnp.float32)).astype(jnp.bfloat16)

    barrier = pltpu.get_barrier_semaphore()
    for other in (after, before, sibling):
        pl.semaphore_signal(barrier, inc=1, device_id=other, device_id_type=pl.DeviceIdType.MESH)
    pl.semaphore_wait(barrier, 3)

    fetch(0, 1).wait()
    relay(0, 0, False)
    fetch(0, 0).wait()
    fetch(1, 1).start()
    fetch(1, 0).start()
    for j in range(own_planes):
        if j + 1 < own_planes:
            relay(0, j + 1, False)
        combine(0, j, True, False)
    fetch(2, 1).start()
    fetch(2, 0).start()
    fetch(1, 1).wait()
    each(lambda j: relay(1, j, False))

    def middle(step, carry):
        fetch(step, 0).wait()
        fetch(step + 1, 1).wait()

        def both(j):
            combine(step, j, False, False)
            relay(step + 1, j, True)

        each(both)

        @pl.when(step + 2 < chips)
        def _fetch():
            fetch(step + 2, 1).start()
            fetch(step + 2, 0).start()

        return carry

    lax.fori_loop(1, chips - 1, middle, 0)
    fetch(chips - 1, 0).wait()
    each(lambda j: combine(chips - 1, j, False, True))
    multiply(place)

    def finish(chunk):
        gram_part(chunk).wait_recv()
        columns = pl.ds(pl.multiple_of(chip_at(chunk) * rows, rows), rows)
        gram[:, columns] += gram_in[chunk]

    def gathered(step, carry):
        def arrive(j):
            gather_arrival(step - 1, j).wait_recv()

            @pl.when(step < chips - 1)
            def _pass_on():
                gather_hop(step, j).start()

        each(arrive)
        multiply(wrap(place - way * step))

        @pl.when(step == chips // 2)
        def _first():
            finish(place)

        @pl.when(step > chips // 2)
        def _met():
            finish(wrap(place - way * step))
            finish(wrap(place - way * (chips - step + 1)))

        return carry

    lax.fori_loop(1, chips, gathered, 0)
    finish(wrap(place - way))

    def drain_gram(chunk, carry):
        gram_part(chunk).wait_send()
        return carry

    lax.fori_loop(0, chips, drain_gram, 0)

    def drain(j, _):
        to_sibling(chips - 2, j).wait_send()
        to_sibling(chips - 1, j).wait_send()

        def sums(step, _):
            hop(step, j).wait_send()
            return _

        lax.fori_loop(0, chips - 1, sums, 0)

        def gather(step, _):
            gather_hop(step, j).wait_send()
            return _

        lax.fori_loop(0, chips - 1, gather, 0)
        return _

    lax.fori_loop(0, own_planes, drain, 0)


def shards(lanes, slab, factor):
    planes = slab.shape[0] * slab.shape[1]
    total_rows, depth = slab.shape[2:]
    ranks = factor.shape[1]
    devices = lax.axis_size("wide")
    chips = devices // HALVES
    rows = total_rows // chips
    own = planes // HALVES
    f32, bf16 = jnp.float32, jnp.bfloat16
    block = (own, rows, ranks)
    dma = pltpu.SemaphoreType.DMA
    return pl.pallas_call(
        functools.partial(kernel, chips, lanes, 1.0 / float(planes * ranks)),
        out_shape=pltpu.VMEM((total_rows // devices, total_rows), f32),
        in_specs=[pl.BlockSpec(memory_space=pl.ANY), pl.BlockSpec(memory_space=pltpu.VMEM)],
        out_specs=pl.BlockSpec(memory_space=pltpu.VMEM),
        scratch_shapes=[
            pltpu.VMEM((2, depth, ranks), bf16),
            pltpu.VMEM((2, 2, own, rows, depth), f32),
            pltpu.VMEM((2,) + block, f32),
            pltpu.VMEM((chips,) + block, f32),
            pltpu.VMEM((chips - 1, own, rows + PEAK_ROWS, ranks), bf16),
            pltpu.VMEM((chips - 1, own, rows + PEAK_ROWS, ranks), bf16),
            pltpu.VMEM((chips,) + block, bf16),
            pltpu.VMEM((chips, rows // HALVES, rows), f32),
            pltpu.VMEM((chips, rows // HALVES, rows), f32),
            dma((2, 2)),
            dma((2, own)),
            dma((chips, own)),
            dma((chips - 1, own)),
            dma((chips - 1, own)),
            dma((chips - 1, own)),
            dma((chips - 1, own)),
            dma((chips,)),
            dma((chips,)),
        ],
        compiler_params=pltpu.CompilerParams(
            collective_id=0, has_side_effects=True, vmem_limit_bytes=54 * 2**20
        ),
        cost_estimate=pl.CostEstimate(
            flops=8 * planes * total_rows * depth * ranks, bytes_accessed=4 * slab.size, transcendentals=0
        ),
    )(slab.reshape(planes, total_rows, depth), factor)


def solution(mesh):
    lanes = 2 if mesh.shape["grp"] == 2 else 1
    placed = (P("grp", None, None, "wide"), P("wide", None))
    return jax.shard_map(
        functools.partial(shards, lanes),
        mesh=mesh, in_specs=placed, out_specs=P(("grp", "wide"), None), check_vma=False,
    )
```
